128 devices in a mesh: rows: 8 (over x, z_lo), cols: 16 (over z_hi, y, core).
Axes of the slice: x: 4, y: 4, z: 4 (z_hi: 2, z_lo: 2; z = z_hi * 2 + z_lo), core: 2. Of those that a mesh axis runs over, the one named last changes fastest.
Arguments:
- spectra: bfloat16 [4096, 4096], P(('rows', 'cols')), may hold values from -6 to 6
- band_weights: float32 [2048], replicated, may hold values from 0.3 to 3
- lag_weights: float32 [4], replicated, may hold values from 0.5 to 2
- selected_bins: int32 [8], replicated, may hold values from 0 to 31
Outputs:
- correlations: float32 [4, 4096, 4096], P(None, 'rows', 'cols')
- gradient: float32 [4096, 4096], P(('rows', 'cols'))
The draws below stay inside these ranges and needn't reach their ends.
All inputs are finite; a program needn't handle non-finite values.
Results may differ from the reference program's by a relative error of at most 0.0045.
Values may be sent and summed in bfloat16 or wider, within the bound.
A program may use at most 128 MiB of HBM per device.

```python
import math
import jax
import jax.numpy as jnp
from jax import lax

F = 2048
LAGS = 4
LAG_STEP = 8
BIN = 128
NSEL = 8
C = 4096
NBIN = 32


def place_ends(array, key, smallest, high):
    longest = array.shape.index(max(array.shape))
    spots = []
    for shift in (0, 1):
        where = [jax.random.randint(jax.random.fold_in(key, axis), (), 0, length) for axis, length in enumerate(array.shape)]
        where[longest] = (where[longest] + shift) % array.shape[longest]
        spots.append(tuple(where))
    return array.at[spots[0]].set(smallest).at[spots[1]].set(high)


def steps_of(own_key, shape, cuts, least, top_value):
    factor_of = 1.0
    for dim, parts in cuts:
        steps = jax.random.uniform(jax.random.fold_in(jax.random.fold_in(own_key, 6), dim), (parts,), jnp.float32, least / len(cuts), top_value / len(cuts))
        factor_of = factor_of * jnp.repeat(jnp.exp(steps), shape[dim] // parts).reshape((-1,) + (1,) * (len(shape) - 1 - dim))
    return factor_of


def noise(key, shape, scale, bound, pieces=(), held_as=jnp.bfloat16):
    values = jax.random.normal(key, shape, jnp.float32) * scale
    if len(pieces) > 0:
        values = steps_of(key, shape, pieces, -0.22, 0.18) * values
    return jnp.clip(values, min=-bound, max=bound).astype(held_as)


def setup_inputs(seed: int = 0) -> dict:
    keys = jax.random.split(jax.random.key(seed), 5)
    return {
        "spectra": noise(keys[0], (C, 2 * F), 1.0, 6.0, ((0, 128),)),
        "band_weights": jnp.clip(jnp.exp(jax.random.uniform(keys[1], (F,), jnp.float32, math.log(0.3), math.log(3.0))), 0.3, 3.0),
        "lag_weights": jnp.clip(jnp.exp(jax.random.uniform(keys[2], (LAGS,), jnp.float32, math.log(0.5), math.log(2.0))), 0.5, 2.0),
        "selected_bins": place_ends(jax.random.randint(keys[3], (NSEL,), 0, NBIN), jax.random.fold_in(keys[3], 1), 0, NBIN - 1).astype(jnp.int32),
    }


def reference(spectra, band_weights, lag_weights, selected_bins):
    raw = spectra.astype(jnp.float32)
    mean_power = lax.optimization_barrier(jnp.mean(raw * raw, axis=1, keepdims=True))
    bin_gains = jnp.concatenate([band_weights, band_weights])
    whitened = (raw * lax.rsqrt(mean_power + 1e-05) * bin_gains[None, :]).astype(jnp.bfloat16)
    channel = jnp.arange(C, dtype=jnp.int32)
    distance = jnp.abs(channel[:, None] - channel[None, :]) // BIN
    chosen = jnp.zeros((C, C), dtype=bool)
    for entry in range(NSEL):
        chosen = jnp.logical_or(chosen, distance == selected_bins[entry])
    selected = chosen.astype(jnp.float32)
    norm_scale = 1.0 / jnp.sqrt(jnp.float32(2 * F))
    bin_index = jnp.arange(F, dtype=jnp.float32)
    real_part = whitened[:, :F].astype(jnp.float32)
    imag_part = whitened[:, F:].astype(jnp.float32)
    outputs = []
    gradient = jnp.zeros((C, 2 * F), jnp.float32)
    for lag_index in range(LAGS):
        shift_lag = float((lag_index - LAGS // 2) * LAG_STEP)
        theta = jnp.pi * bin_index * shift_lag / F
        cosine = jnp.cos(theta)
        sine_part = jnp.sin(theta)
        rotated = jnp.concatenate([real_part * cosine - imag_part * sine_part, imag_part * cosine + real_part * sine_part], axis=1).astype(jnp.bfloat16)
        correlation = jnp.dot(rotated, whitened.T, preferred_element_type=jnp.float32) * norm_scale
        outputs.append(correlation)
        adjoint = (lag_weights[lag_index] * selected * correlation).astype(jnp.bfloat16)
        back = jnp.dot(adjoint, whitened, preferred_element_type=jnp.float32) * norm_scale
        back_real = back[:, :F]
        back_imag = back[:, F:]
        gradient = gradient + jnp.concatenate([back_real * cosine + back_imag * sine_part, back_imag * cosine - back_real * sine_part], axis=1)
        gradient = gradient + jnp.dot(adjoint.T, rotated, preferred_element_type=jnp.float32) * norm_scale
    return (jnp.stack(outputs), gradient)
```

```python
import functools

import jax
import jax.numpy as jnp
import numpy as np
from jax import lax
from jax.experimental import pallas as pl
from jax.experimental.pallas import tpu as pltpu
from jax.sharding import PartitionSpec as P

MESH = pl.DeviceIdType.MESH
LAG_STEP = 8
BIN = 128
NSEL = 8
NA = 5
C = 4096
F = 2048
NP = 4
B = F // NP
B2 = 2 * B
CH = 32
TR = 2 * 4 * 2 * CH
TC = 4 * 2 * CH
EPS = 1e-05
SCALE = 1.0 / np.sqrt(2.0 * F)

ZX, YP, YM, YFP, YFM, SB = 0, 1, 2, 3, 4, 5
PM, ZL, XP, XM, XFP, XFM = 6, 7, 8, 9, 10, 11
GS, G1P, G1M, G2P, G2M, G3 = 12, 13, 14, 15, 16, 17
NK = 18


def tables():
    theta = np.pi * np.arange(F) * LAG_STEP / F
    rows = np.stack([np.cos(theta), np.sin(theta), np.cos(2 * theta), np.sin(2 * theta)])
    return rows.reshape(4, NP, 1, B).transpose(1, 0, 2, 3).astype(np.float32)


def kernel(
    lagw_ref, bins_ref, spec_ref, gain_ref, tab_ref, corr_ref, grad_ref,
    row, col, acc, sel, adj, part, s_gs, r_gs, s_g1, r_g1, s_g2, r_g2, s_g3, r_g3, fin,
    ssem, rsem, osem,
):
    r = lax.axis_index("rows")
    c = lax.axis_index("cols")
    x, zl, zh, y, k = r // 2, r % 2, c // 8, (c // 2) % 4, c % 2
    y1, y2, y3 = (y + 1) % 4, (y + 2) % 4, (y + 3) % 4
    x1, x3 = (x + 1) % 4, (x + 3) % 4

    def at(x_, zl_, zh_, y_, k_):
        return (x_ * 2 + zl_, zh_ * 8 + y_ * 2 + k_)

    xs, zs = c // 4, (c // 2) % 2
    yy = (x - xs + 4) % 4
    kk = (zl + zs + k + 1) % 2
    yy1, yy2, yy3 = (yy + 1) % 4, (yy + 2) % 4, (yy + 3) % 4
    to_perm = at((y + x) % 4, (zl + k + zh + 1) % 2, r // 4, r % 4, zh)
    from_perm = at(xs, zs, k, yy, kk)
    d_zx = at(x, zl, 1 - zh, y, k)
    d_yp = at(x, zl, zh, y1, k)
    d_ym = at(x, zl, zh, y3, k)
    d_sb = at(x, zl, zh, y, 1 - k)
    d_zl = at(x, 1 - zl, zh, y, k)
    d_xp = at(x1, zl, zh, y, k)
    d_xm = at(x3, zl, zh, y, k)

    barrier = pltpu.get_barrier_semaphore()
    both = (d_zx, d_yp, d_ym, d_sb, d_zl, d_xp, d_xm)
    for d in both + (from_perm,):
        pl.semaphore_signal(barrier, inc=1, device_id=d, device_id_type=MESH)

    raw = spec_ref[...].astype(jnp.float32)
    power = jnp.mean(raw * raw, axis=1, keepdims=True)
    inv = lax.rsqrt(power + EPS)
    for p in range(NP):
        for h in range(2):
            s = slice(h * F + p * B, h * F + (p + 1) * B)
            g = gain_ref[:, p * B : (p + 1) * B]
            v = spec_ref[:, s].astype(jnp.float32) * inv * g
            row[p, zh, y, k, :, h * B : (h + 1) * B] = v.astype(jnp.bfloat16)

    pl.semaphore_wait(barrier, len(both) + 1)

    def send(kind, p, src, dst, dev):
        pltpu.make_async_remote_copy(
            src_ref=src, dst_ref=dst, send_sem=ssem.at[kind, p], recv_sem=rsem.at[kind, p],
            device_id=dev, device_id_type=MESH,
        ).start()

    def got(kind, p, dst):
        pltpu.make_async_copy(dst, dst, rsem.at[kind, p]).wait()

    def sent(kind, p, src):
        pltpu.make_async_copy(src, src, ssem.at[kind, p]).wait()

    for p in range(NP):
        own = row.at[p, zh, y, k]
        send(ZX, p, own, own, d_zx)
        send(PM, p, own, col.at[p, 2, y, k], to_perm)

    bits = jnp.int32(0)
    for e in range(NSEL):
        bits = bits | (jnp.int32(1) << bins_ref[e])

    def mask_rows(i, carry):
        ri = r * TR + i * 64 + lax.broadcasted_iota(jnp.int32, (64, TC), 0)
        ci = c * TC + lax.broadcasted_iota(jnp.int32, (64, TC), 1)
        dist = lax.shift_right_logical(jnp.abs(ri - ci), 7)
        hit = lax.shift_right_logical(jnp.full((64, TC), bits, jnp.int32), dist) & 1
        sel[pl.ds(pl.multiple_of(i * 64, 64), 64), :] = hit.astype(jnp.float32)
        return carry

    lax.fori_loop(0, TR // 64, mask_rows, 0)

    def stage1(p):
        got(PM, p, col.at[p, 2, yy, kk])
        mine = col.at[p, 2, yy, kk]
        send(ZL, p, mine, mine, d_zl)
        got(ZX, p, row.at[p, 1 - zh, y, k])
        mine = row.at[p, :, y, k]
        send(YP, p, mine, mine, d_yp)
        send(YM, p, mine, mine, d_ym)
        got(ZL, p, col.at[p, 2, yy, 1 - kk])
        mine = col.at[p, 2, yy]
        send(XP, p, mine, mine, d_xp)
        send(XM, p, mine, mine, d_xm)

    def stage2(p):
        got(YP, p, row.at[p, :, y3, k])
        blk = row.at[p, 0, y3, k]
        send(YFP, p, blk, blk, d_yp)
        got(YM, p, row.at[p, :, y1, k])
        blk = row.at[p, 1, y1, k]
        send(YFM, p, blk, blk, d_ym)
        got(XP, p, col.at[p, 2, yy3])
        blk = col.at[p, 2, yy3, 0]
        send(XFP, p, blk, blk, d_xp)
        got(XM, p, col.at[p, 2, yy1])
        blk = col.at[p, 2, yy1, 1]
        send(XFM, p, blk, blk, d_xm)

    def stage3(p):
        got(YFP, p, row.at[p, 0, y2, k])
        got(YFM, p, row.at[p, 1, y2, k])
        blk = row.at[p, :, :, k]
        send(SB, p, blk, blk, d_sb)
        got(XFP, p, col.at[p, 2, yy2, 0])
        got(XFM, p, col.at[p, 2, yy2, 1])

        def rot(i, carry):
            a, b = i // 2, i % 2
            v = col[p, 2, a, b]
            re = v[:, :B].astype(jnp.float32)
            im = v[:, B:].astype(jnp.float32)
            for t, (near, far) in enumerate(((1, 3), (0, 4))):
                cs = tab_ref[p, 2 * t]
                sn = tab_ref[p, 2 * t + 1]
                rc, rs, ic, is_ = re * cs, re * sn, im * cs, im * sn
                col[p, far, a, b, :, :B] = (rc + is_).astype(jnp.bfloat16)
                col[p, far, a, b, :, B:] = (ic - rs).astype(jnp.bfloat16)
                col[p, near, a, b, :, :B] = (rc - is_).astype(jnp.bfloat16)
                col[p, near, a, b, :, B:] = (ic + rs).astype(jnp.bfloat16)
            return carry

        lax.fori_loop(0, 8, rot, 0)

    def stage4(p):
        got(SB, p, row.at[p, :, :, 1 - k])

        def corr(a, carry):
            left = row[p].reshape(TR, B2)
            right = col[p, a].reshape(TC, B2)
            d = lax.dot_general(
                left, right, (((1,), (1,)), ((), ())), preferred_element_type=jnp.float32
            )
            if p == 0:
                acc[a] = d
            else:
                acc[a] += d
            return carry

        lax.fori_loop(0, NA, corr, 0)

    for t in range(NP + 3):
        for lag, stage in enumerate((stage1, stage2, stage3, stage4)):
            if 0 <= t - lag < NP:
                stage(t - lag)

    w0, w8, w16 = 2.0 * lagw_ref[2], lagw_ref[1] + lagw_ref[3], lagw_ref[0]
    for a, w in enumerate((w16, w8, w0, w8, w16)):

        def adjoint(i, carry):
            rows = pl.ds(pl.multiple_of(i * 64, 64), 64)
            v = acc[a, rows, :] * jnp.float32(SCALE)
            if a < 4:
                acc[a, rows, :] = v
            adj[rows, a * TC : (a + 1) * TC] = (v * (sel[rows, :] * w)).astype(jnp.bfloat16)
            return carry

        lax.fori_loop(0, TR // 64, adjoint, 0)
    outs = [pltpu.make_async_copy(acc.at[a], corr_ref.at[a], osem.at[a]) for a in range(4)]
    for o in outs:
        o.start()

    def grad0(p):
        def tile(n, carry):
            cols = pl.ds(pl.multiple_of(n * 256, 256), 256)
            d = jnp.dot(
                adj[...], col[p, :, :, :, :, cols].reshape(NA * TC, 256),
                preferred_element_type=jnp.float32,
            )
            part[p, :, :, :, :, cols] = d.reshape(2, 4, 2, CH, 256)
            return carry

        lax.fori_loop(0, B2 // 256, tile, 0)
        s_gs[p] = part[p, :, :, 1 - k].astype(jnp.bfloat16)
        send(GS, p, s_gs.at[p], r_gs.at[p], d_sb)

    def mine_at(p, h, yt):
        return part[p, h, yt, k] + r_gs[p, h, yt].astype(jnp.float32)

    def grad1(p):
        got(GS, p, r_gs.at[p])
        s_g1[p, 0] = mine_at(p, 0, y2).astype(jnp.bfloat16)
        send(G1P, p, s_g1.at[p, 0], r_g1.at[p, 0], d_yp)
        s_g1[p, 1] = mine_at(p, 1, y2).astype(jnp.bfloat16)
        send(G1M, p, s_g1.at[p, 1], r_g1.at[p, 1], d_ym)

    def grad2(p):
        got(G1P, p, r_g1.at[p, 0])
        s_g2[p, 0, 0] = (mine_at(p, 0, y1) + r_g1[p, 0].astype(jnp.float32)).astype(jnp.bfloat16)
        s_g2[p, 0, 1] = mine_at(p, 1, y1).astype(jnp.bfloat16)
        send(G2P, p, s_g2.at[p, 0], r_g2.at[p, 0], d_yp)
        got(G1M, p, r_g1.at[p, 1])
        s_g2[p, 1, 0] = mine_at(p, 0, y3).astype(jnp.bfloat16)
        s_g2[p, 1, 1] = (mine_at(p, 1, y3) + r_g1[p, 1].astype(jnp.float32)).astype(jnp.bfloat16)
        send(G2M, p, s_g2.at[p, 1], r_g2.at[p, 1], d_ym)

    def total_at(p, h):
        return (
            mine_at(p, h, y)
            + r_g2[p, 0, h].astype(jnp.float32)
            + r_g2[p, 1, h].astype(jnp.float32)
        )

    def grad3(p):
        got(G2P, p, r_g2.at[p, 0])
        got(G2M, p, r_g2.at[p, 1])
        s_g3[p] = total_at(p, 1 - zh).astype(jnp.bfloat16)
        send(G3, p, s_g3.at[p], r_g3.at[p], d_zx)
        fin[p] = total_at(p, zh)

    def grad4(p):
        got(G3, p, r_g3.at[p])
        v = (fin[p] + r_g3[p].astype(jnp.float32)) * jnp.float32(SCALE)
        grad_ref[:, p * B : (p + 1) * B] = v[:, :B]
        grad_ref[:, F + p * B : F + (p + 1) * B] = v[:, B:]

    for t in range(NP + 4):
        for lag, stage in enumerate((grad0, grad1, grad2, grad3, grad4)):
            if 0 <= t - lag < NP:
                stage(t - lag)

    for p in range(NP):
        for kind, src in (
            (ZX, row.at[p, zh, y, k]), (PM, row.at[p, zh, y, k]),
            (YP, row.at[p, :, y, k]), (YM, row.at[p, :, y, k]),
            (YFP, row.at[p, 0, y3, k]), (YFM, row.at[p, 1, y1, k]),
            (SB, row.at[p, :, :, k]), (ZL, col.at[p, 2, yy, kk]),
            (XP, col.at[p, 2, yy]), (XM, col.at[p, 2, yy]),
            (XFP, col.at[p, 2, yy3, 0]), (XFM, col.at[p, 2, yy1, 1]),
            (GS, s_gs.at[p]), (G1P, s_g1.at[p, 0]), (G1M, s_g1.at[p, 1]),
            (G2P, s_g2.at[p, 0]), (G2M, s_g2.at[p, 1]), (G3, s_g3.at[p]),
        ):
            sent(kind, p, src)
    for o in outs:
        o.wait()


def per_device(spectra, band_weights, lag_weights, selected_bins):
    bf16, f32 = jnp.bfloat16, jnp.float32
    smem = pl.BlockSpec(memory_space=pltpu.SMEM)
    vmem = pl.BlockSpec(memory_space=pltpu.VMEM)
    return pl.pallas_call(
        kernel,
        out_shape=(
            jax.ShapeDtypeStruct((4, TR, TC), f32),
            jax.ShapeDtypeStruct((CH, 2 * F), f32),
        ),
        in_specs=[smem, smem, vmem, vmem, vmem],
        out_specs=(pl.BlockSpec(memory_space=pl.ANY), vmem),
        scratch_shapes=[
            pltpu.VMEM((NP, 2, 4, 2, CH, B2), bf16),
            pltpu.VMEM((NP, NA, 4, 2, CH, B2), bf16),
            pltpu.VMEM((NA, TR, TC), f32),
            pltpu.VMEM((TR, TC), f32),
            pltpu.VMEM((TR, NA * TC), bf16),
            pltpu.VMEM((NP, 2, 4, 2, CH, B2), f32),
            pltpu.VMEM((NP, 2, 4, CH, B2), bf16),
            pltpu.VMEM((NP, 2, 4, CH, B2), bf16),
            pltpu.VMEM((NP, 2, CH, B2), bf16),
            pltpu.VMEM((NP, 2, CH, B2), bf16),
            pltpu.VMEM((NP, 2, 2, CH, B2), bf16),
            pltpu.VMEM((NP, 2, 2, CH, B2), bf16),
            pltpu.VMEM((NP, CH, B2), bf16),
            pltpu.VMEM((NP, CH, B2), bf16),
            pltpu.VMEM((NP, CH, B2), f32),
            pltpu.SemaphoreType.DMA((NK, NP)),
            pltpu.SemaphoreType.DMA((NK, NP)),
            pltpu.SemaphoreType.DMA((4,)),
        ],
        compiler_params=pltpu.CompilerParams(
            collective_id=0, has_side_effects=True, vmem_limit_bytes=60 * 2**20
        ),
        cost_estimate=pl.CostEstimate(
            flops=4 * TR * TC * NA * 2 * F, bytes_accessed=4 * TR * TC * 4, transcendentals=0
        ),
        name="noise_corr",
    )(lag_weights, selected_bins, spectra, band_weights.reshape(1, F), jnp.asarray(tables()))


def solution(mesh):
    placed = (P(("rows", "cols"), None), P(), P(), P())
    return jax.shard_map(
        per_device,
        mesh=mesh,
        in_specs=placed,
        out_specs=(P(None, "rows", "cols"), P(("rows", "cols"), None)),
        check_vma=False,
    )
```

```python
import functools

import jax
import jax.numpy as jnp
import numpy as np
from jax import lax
from jax.experimental import pallas as pl
from jax.experimental.pallas import tpu as pltpu
from jax.sharding import PartitionSpec as P

MESH = pl.DeviceIdType.MESH
LAG_STEP = 8
BIN = 128
NSEL = 8
NA = 5
C = 4096
F = 2048
NP = 4
B = F // NP
B2 = 2 * B
CH = 32
TR = 2 * 4 * 2 * CH
TC = 4 * 2 * CH
EPS = 1e-05
SCALE = 1.0 / np.sqrt(2.0 * F)

NPC = NP // 2

TURN = (0, 1, 4, 2, 3)

GROUPS = {
    "ZX": "ZX", "YPO": "YO", "YMO": "YO", "YPQ": "YQ", "YMQ": "YQ", "YFO": "YF", "YFQ": "YF",
    "SB": "SB", "PM": "PM", "ZL": "ZL", "XPO": "XO", "XMO": "XO", "XPQ": "XQ", "XMQ": "XQ",
    "XFO": "XF", "XFQ": "XF", "GS": "GS", "G1P": "G1", "G1M": "G1", "G2P0": "G2", "G2P1": "G2",
    "G2M0": "G2", "G2M1": "G2", "G3": "G3", "H1P": "H1", "H1M": "H1", "H2PO": "H2",
    "H2PQ": "H2", "H2MO": "H2", "H2MQ": "H2", "H4O": "H4", "H4Q": "H4", "H5": "H5",
}
KINDS = list(GROUPS)
ARRIVALS = sorted(set(GROUPS.values()))
NK, NG = len(KINDS), len(ARRIVALS)


def tables():
    theta = np.pi * np.arange(F) * LAG_STEP / F
    rows = np.stack([np.cos(theta), np.sin(theta), np.cos(2 * theta), np.sin(2 * theta)])
    return rows.reshape(4, NP, 1, B).transpose(1, 0, 2, 3).astype(np.float32)


def kernel(
    lagw_in, bins_in, spec_in, gain_in, tab_in, corr_ref, grad_ref,
    row, col, turned, acc, sel, adj, adjt, part, partc,
    s_gs, r_gs, s_g1, r_g1, s_g2, r_g2, s_g3, r_g3, fin,
    s_h1, r_h1, s_h2, r_h2, s_h4, r_h4, s_h5, r_h5, lagw_ref, bins_ref, spec_ref, gain_ref, tab_ref,
    ssem, rsem, hsem, osem, isem,
):
    ins = [
        pltpu.make_async_copy(src, dst, isem.at[i])
        for i, (src, dst) in enumerate((
            (spec_in, spec_ref), (gain_in, gain_ref), (bins_in, bins_ref),
            (lagw_in, lagw_ref), (tab_in, tab_ref),
        ))
    ]
    for copy in ins:
        copy.start()
    r = lax.axis_index("rows")
    c = lax.axis_index("cols")
    x, zl, zh, y, k = r // 2, r % 2, c // 8, (c // 2) % 4, c % 2
    y1, y2, y3 = (y + 1) % 4, (y + 2) % 4, (y + 3) % 4
    x1, x3 = (x + 1) % 4, (x + 3) % 4

    def at(x_, zl_, zh_, y_, k_):
        return (x_ * 2 + zl_, zh_ * 8 + y_ * 2 + k_)

    xs, zs = c // 4, (c // 2) % 2
    kk = (zl + zs + k + 1) % 2
    yy = (x + 15 - k - 2 * kk - 3 * (xs // 2)) % 4
    yy1, yy2, yy3 = (yy + 1) % 4, (yy + 2) % 4, (yy + 3) % 4
    xt, zt = (y + zh + 2 * k + 3 * (x // 2) + 1) % 4, (zl + k + zh) % 2
    to_perm, from_perm = at(xt, 1 - zt, r // 4, r % 4, zh), at(xs, zs, k, yy, kk)
    to_mid = [at(x, zs, k, v, (k + 1 + y // 2 + v // 2) % 2) for v in (yy, yy2)]
    turn = (x + 7 - zh - y) % 4
    zm = turn % 2
    km = ((turn + 4 - 3 * zm) % 4) // 2
    ym = 2 * ((k + zh + 1 + y // 2) % 2) + zl
    xm = 2 * zm + ym // 2
    from_rep = [at(x, h, zm, ym, zh) for h in range(2)]
    home = at(xm, zl, zh, y, km)
    at_home = (xm == x) & (km == k)
    from_mid = at(xt, zl, zh, y, (zh + 1 + (r % 4) // 2 + y // 2) % 2)
    via_self = (xt == x) & ((zh + 1 + (r % 4) // 2 + y // 2) % 2 == k)
    d_zx = at(x, zl, 1 - zh, y, k)
    d_yp = at(x, zl, zh, y1, k)
    d_ym = at(x, zl, zh, y3, k)
    d_sb = at(x, zl, zh, y, 1 - k)
    d_zl = at(x, 1 - zl, zh, y, k)
    d_xp = at(x1, zl, zh, y, k)
    d_xm = at(x3, zl, zh, y, k)
    ysrc, ydst = (y + 3 + 2 * zh) % 4, (y + 1 + 2 * zh) % 4
    xsrc, xdst = (x + 3 + 2 * kk) % 4, (x + 1 + 2 * kk) % 4
    yysrc = (yy + 3 + 2 * kk) % 4
    d_ys, d_yd = at(x, zl, zh, ysrc, k), at(x, zl, zh, ydst, k)
    d_xs, d_xd = at(xsrc, zl, zh, y, k), at(xdst, zl, zh, y, k)

    barrier = pltpu.get_barrier_semaphore()
    peers = [d_zx, d_yp, d_ym, d_sb, d_zl, d_xp, d_xm, from_perm] + from_rep
    for d in peers:
        pl.semaphore_signal(barrier, inc=1, device_id=d, device_id_type=MESH)

    @pl.when(jnp.logical_not(via_self))
    def _():
        pl.semaphore_signal(barrier, inc=1, device_id=from_mid, device_id_type=MESH)

    for copy in ins:
        copy.wait()
    raw = spec_ref[...].astype(jnp.float32)
    power = jnp.mean(raw * raw, axis=1, keepdims=True)
    inv = lax.rsqrt(power + EPS)
    for p in range(NP):
        for h in range(2):
            s = slice(h * F + p * B, h * F + (p + 1) * B)
            g = gain_ref[:, p * B : (p + 1) * B]
            v = spec_ref[:, s].astype(jnp.float32) * inv * g
            row[p, zh, y, k, :, h * B : (h + 1) * B] = v.astype(jnp.bfloat16)

    pl.semaphore_wait(barrier, jnp.where(at_home, len(peers), len(peers) + 1))

    def send(kind, p, src, dst, dev):
        i = KINDS.index(kind)
        pltpu.make_async_remote_copy(
            src_ref=src, dst_ref=dst, send_sem=ssem.at[i],
            recv_sem=rsem.at[ARRIVALS.index(GROUPS[kind]), p],
            device_id=dev, device_id_type=MESH,
        ).start()

    def got(group, p, dst):
        pltpu.make_async_copy(dst, dst, rsem.at[ARRIVALS.index(group), p]).wait()

    def sent(kinds, src):
        for kind in kinds:
            pltpu.make_async_copy(src, src, ssem.at[KINDS.index(kind)]).wait()

    def run(count, table):
        for t in range(count + max(skew for _, skew in table)):
            for fn, skew in table:
                if 0 <= t - skew < count:
                    fn(t - skew)

    bits = jnp.int32(0)
    for e in range(NSEL):
        bits = bits | (jnp.int32(1) << bins_ref[e])

    def mask(p):
        def mask_rows(i, carry):
            ri = r * TR + i * 64 + lax.broadcasted_iota(jnp.int32, (64, TC), 0)
            ci = c * TC + lax.broadcasted_iota(jnp.int32, (64, TC), 1)
            dist = lax.shift_right_logical(jnp.abs(ri - ci), 7)
            hit = lax.shift_right_logical(jnp.full((64, TC), bits, jnp.int32), dist) & 1
            sel[pl.ds(pl.multiple_of(i * 64, 64), 64), :] = hit.astype(jnp.float32)
            return carry

        if p == NP - 1:
            lax.fori_loop(0, TR // 64, mask_rows, 0)

    def pair(kind, p, blk, *devs):
        for way, dev in zip("PM", devs):
            send(kind[0] + way + kind[1], p, blk, blk, dev)

    def s_start(p):
        own = row.at[p, zh, y, k]
        send("PM", p, own, col.at[p, 2, y, k], to_perm)
        send("ZX", p, own, own, d_zx)
        pair("YO", p, own, d_yp, d_ym)

    def s_perm(p):
        blk = col.at[p, 2, yy, kk]
        got("PM", p, blk)
        send("ZL", p, blk, blk, d_zl)
        pair("XO", p, blk, d_xp, d_xm)

    def s_zx(p):
        blk = row.at[p, 1 - zh, y, k]
        got("ZX", p, blk)
        pair("YQ", p, blk, d_yp, d_ym)

    def s_zl(p):
        blk = col.at[p, 2, yy2, 1 - kk]
        got("ZL", p, blk)
        pair("XQ", p, blk, d_xp, d_xm)

    def f_yo(p):
        got("YO", p, row.at[p, :, y1, k])
        blk = row.at[p, zh, ysrc, k]
        send("YFO", p, blk, blk, d_yd)

    def f_xo(p):
        got("XO", p, col.at[p, 2, yy1])
        blk = col.at[p, 2, yysrc, kk]
        send("XFO", p, blk, blk, d_xd)

    def f_yq(p):
        got("YQ", p, row.at[p, :, y1, k])
        blk = row.at[p, 1 - zh, ydst, k]
        send("YFQ", p, blk, blk, d_ys)

    def f_xq(p):
        got("XQ", p, col.at[p, 2, yy1])
        blk = col.at[p, 2, yysrc, 1 - kk]
        send("XFQ", p, blk, blk, d_xs)

    def s_sib(p):
        got("YF", p, row.at[p, :, y2, k])
        blk = row.at[p, :, :, k]
        send("SB", p, blk, blk, d_sb)

    def g_xf(p):
        got("XF", p, col.at[p, 2, yy2])

    def g_sib(p):
        got("SB", p, row.at[p, :, :, 1 - k])

    def rotate(p, v, put):
        re = v[:, :B].astype(jnp.float32)
        im = v[:, B:].astype(jnp.float32)
        for t in range(2):
            cs, sn = tab_ref[p, 2 * t], tab_ref[p, 2 * t + 1]
            rc, rs, ic, is_ = re * cs, re * sn, im * cs, im * sn
            put(t, 0, (rc - is_).astype(jnp.bfloat16), (ic + rs).astype(jnp.bfloat16))
            put(t, 1, (rc + is_).astype(jnp.bfloat16), (ic - rs).astype(jnp.bfloat16))

    def rot(p):
        def body(i, carry):
            a, b = i // 2, i % 2

            def put(t, back, re, im):
                o = ((1, 3), (0, 4))[t][back]
                col[p, o, a, b, :, :B] = re
                col[p, o, a, b, :, B:] = im

            rotate(p, col[p, 2, a, b], put)
            return carry

        lax.fori_loop(0, 8, body, 0)

    def rot_first(p):
        def body(i, carry):
            h, a, b = i // 8, (i // 2) % 4, i % 2

            def put(t, back, re, im):
                o = ((2, 1), (3, 0))[t][back]
                turned[p, o, h, a, b, :, :B] = re
                turned[p, o, h, a, b, :, B:] = im

            rotate(p, row[p, h, a, b], put)
            return carry

        if p < NPC:
            lax.fori_loop(0, 16, body, 0)

    def correlate(p):
        left = row[p].reshape(TR, B2)
        for a in range(NA):
            d = lax.dot_general(
                left, col[p, a].reshape(TC, B2), (((1,), (1,)), ((), ())),
                preferred_element_type=jnp.float32,
            )
            if p > 0:
                d = acc[a] + d
            if p < NP - 1:
                acc[a] = d
                continue
            d = d * jnp.float32(SCALE)
            if a < 4:
                acc[a] = d
                outs[a].start()
            d = (d * (sel[...] * weights[a])).astype(jnp.bfloat16)
            adj[:, a * TC : (a + 1) * TC] = d
            adjt[TURN[a] * TR : (TURN[a] + 1) * TR, :] = d

    outs = [pltpu.make_async_copy(acc.at[a], corr_ref.at[a], osem.at[a]) for a in range(4)]
    w0, w8, w16 = 2.0 * lagw_ref[2], lagw_ref[1] + lagw_ref[3], lagw_ref[0]
    weights = (w16, w8, w0, w8, w16)
    run(NP, [
        (s_start, 0), (mask, 0), (s_perm, 1), (s_zx, 1), (f_yo, 1), (s_zl, 2), (f_xo, 2), (f_yq, 2),
        (f_xq, 3), (s_sib, 3), (g_xf, 4), (rot, 4), (g_sib, 4), (correlate, 4), (rot_first, 4),
    ])

    def f32(v):
        return v.astype(jnp.float32)

    def b16(v):
        return v.astype(jnp.bfloat16)

    def grad0(q):
        p = NPC + q

        d = jnp.dot(
            adj[...], col[p].reshape(NA * TC, B2), preferred_element_type=jnp.float32
        )
        part[q] = d.reshape(2, 4, 2, CH, B2)
        s_gs[q] = b16(part[q, :, :, 1 - k])
        send("GS", q, s_gs.at[q], r_gs.at[q], d_sb)

    def mine_at(q, h, yt):
        return part[q, h, yt, k] + f32(r_gs[q, h, yt])

    def reach(kind, q, src, dst, value, dev):
        src[...] = b16(value)
        send(kind, q, src, dst, dev)

    def grad1(q):
        got("GS", q, r_gs.at[q])
        reach("G1P", q, s_g1.at[q, 0], r_g1.at[q, 0], mine_at(q, 0, y2), d_yp)
        reach("G1M", q, s_g1.at[q, 1], r_g1.at[q, 1], mine_at(q, 1, y2), d_ym)
        reach("G2P1", q, s_g2.at[q, 0, 1], r_g2.at[q, 0, 1], mine_at(q, 1, y1), d_yp)
        reach("G2M0", q, s_g2.at[q, 1, 0], r_g2.at[q, 1, 0], mine_at(q, 0, y3), d_ym)

    def grad2(q):
        got("G1", q, r_g1.at[q])
        v = mine_at(q, 0, y1) + f32(r_g1[q, 0])
        reach("G2P0", q, s_g2.at[q, 0, 0], r_g2.at[q, 0, 0], v, d_yp)
        v = mine_at(q, 1, y3) + f32(r_g1[q, 1])
        reach("G2M1", q, s_g2.at[q, 1, 1], r_g2.at[q, 1, 1], v, d_ym)

    def grad3(q):
        def total_at(h):
            return mine_at(q, h, y) + f32(r_g2[q, 0, h]) + f32(r_g2[q, 1, h])

        got("G2", q, r_g2.at[q])
        s_g3[q] = b16(total_at(1 - zh))
        send("G3", q, s_g3.at[q], r_g3.at[q], d_zx)
        fin[q] = total_at(zh)

    def put_grad(p, v):
        v = v * jnp.float32(SCALE)
        grad_ref[:, p * B : (p + 1) * B] = v[:, :B]
        grad_ref[:, F + p * B : F + (p + 1) * B] = v[:, B:]

    def grad4(q):
        got("G3", q, r_g3.at[q])
        put_grad(NPC + q, fin[q] + f32(r_g3[q]))

    def colg0(q):
        def turned_dot(lags, right):
            return lax.dot_general(
                lags, right, (((0,), (0,)), ((), ())), preferred_element_type=jnp.float32
            )

        d = turned_dot(adjt[: 4 * TR, :], turned[q].reshape(4 * TR, B2))
        d += turned_dot(adjt[4 * TR :, :], row[q].reshape(TR, B2))
        partc[q] = d.reshape(4, 2, CH, B2)
        reach("H1P", q, s_h1.at[q, 0], r_h1.at[q, 0], partc[q, yy2, kk], d_xp)
        reach("H1M", q, s_h1.at[q, 1], r_h1.at[q, 1], partc[q, yy, 1 - kk], d_xm)
        reach("H2PQ", q, s_h2.at[q, 0, 1], r_h2.at[q, 0, 1], partc[q, yy3, 1 - kk], d_xp)
        reach("H2MO", q, s_h2.at[q, 1, 0], r_h2.at[q, 1, 0], partc[q, yy3, kk], d_xm)

    def colg1(q):
        got("H1", q, r_h1.at[q])
        v = partc[q, yy1, kk] + f32(r_h1[q, 0])
        reach("H2PO", q, s_h2.at[q, 0, 0], r_h2.at[q, 0, 0], v, d_xp)
        v = partc[q, yy1, 1 - kk] + f32(r_h1[q, 1])
        reach("H2MQ", q, s_h2.at[q, 1, 1], r_h2.at[q, 1, 1], v, d_xm)

    def colg2(q):
        got("H2", q, r_h2.at[q])
        v = partc[q, yy, kk] + f32(r_h2[q, 0, 0]) + f32(r_h2[q, 1, 0])
        reach("H4O", q, s_h4.at[q, 0], r_h4.at[q, 0], v, to_mid[0])
        v = partc[q, yy2, 1 - kk] + f32(r_h2[q, 0, 1]) + f32(r_h2[q, 1, 1])
        reach("H4Q", q, s_h4.at[q, 1], r_h4.at[q, 1], v, to_mid[1])

    def homeward(q):
        return pltpu.make_async_remote_copy(
            src_ref=s_h5.at[q], dst_ref=r_h5.at[q], send_sem=hsem.at[q],
            recv_sem=rsem.at[ARRIVALS.index("H5"), q], device_id=home, device_id_type=MESH,
        )

    def colg3(q):
        got("H4", q, r_h4.at[q])
        s_h5[q] = b16(f32(r_h4[q, 0]) + f32(r_h4[q, 1]))

        @pl.when(at_home)
        def _():
            r_h5[q] = s_h5[q]

        @pl.when(jnp.logical_not(at_home))
        def _():
            homeward(q).start()

    def colg4(q):
        @pl.when(jnp.logical_not(at_home))
        def _():
            homeward(q).wait_send()

        @pl.when(jnp.logical_not(via_self))
        def _():
            got("H5", q, r_h5.at[q])

        put_grad(q, f32(r_h5[q]))

    def settle():
        for kind in KINDS[: KINDS.index("GS")]:
            sent([kind], row.at[:, :, :, k] if kind == "SB" else row.at[:, zh, y, k])
        for o in outs:
            o.wait()

    for q in range(NPC):
        colg0(q)
        grad0(q)
    for n, fns in enumerate(((colg1, grad1), (colg2, grad2), (colg3, grad3), (colg4, grad4))):
        for q in range(NPC):
            for fn in fns:
                fn(q)
        if n == 0:
            settle()

    for kind in KINDS[KINDS.index("GS") : KINDS.index("H5")]:
        sent([kind], s_gs if kind == "GS" else s_h1.at[:, 0])


def per_device(spectra, band_weights, lag_weights, selected_bins):
    bf16, f32 = jnp.bfloat16, jnp.float32
    hbm = pl.BlockSpec(memory_space=pltpu.HBM)
    vmem = pl.BlockSpec(memory_space=pltpu.VMEM)
    return pl.pallas_call(
        kernel,
        out_shape=(
            jax.ShapeDtypeStruct((4, TR, TC), f32),
            jax.ShapeDtypeStruct((CH, 2 * F), f32),
        ),
        in_specs=[hbm] * 5,
        out_specs=(pl.BlockSpec(memory_space=pl.ANY), vmem),
        scratch_shapes=[
            pltpu.VMEM((NP, 2, 4, 2, CH, B2), bf16),
            pltpu.VMEM((NP, NA, 4, 2, CH, B2), bf16),
            pltpu.VMEM((NPC, 4, 2, 4, 2, CH, B2), bf16),
            pltpu.VMEM((NA, TR, TC), f32),
            pltpu.VMEM((TR, TC), f32),
            pltpu.VMEM((TR, NA * TC), bf16),
            pltpu.VMEM((NA * TR, TC), bf16),
            pltpu.VMEM((NPC, 2, 4, 2, CH, B2), f32),
            pltpu.VMEM((NPC, 4, 2, CH, B2), f32),
            pltpu.VMEM((NPC, 2, 4, CH, B2), bf16),
            pltpu.VMEM((NPC, 2, 4, CH, B2), bf16),
            pltpu.VMEM((NPC, 2, CH, B2), bf16),
            pltpu.VMEM((NPC, 2, CH, B2), bf16),
            pltpu.VMEM((NPC, 2, 2, CH, B2), bf16),
            pltpu.VMEM((NPC, 2, 2, CH, B2), bf16),
            pltpu.VMEM((NPC, CH, B2), bf16),
            pltpu.VMEM((NPC, CH, B2), bf16),
            pltpu.VMEM((NPC, CH, B2), f32),
            pltpu.VMEM((NPC, 2, CH, B2), bf16),
            pltpu.VMEM((NPC, 2, CH, B2), bf16),
            pltpu.VMEM((NPC, 2, 2, CH, B2), bf16),
            pltpu.VMEM((NPC, 2, 2, CH, B2), bf16),
            pltpu.VMEM((NPC, 2, CH, B2), bf16),
            pltpu.VMEM((NPC, 2, CH, B2), bf16),
            pltpu.VMEM((NPC, CH, B2), bf16),
            pltpu.VMEM((NPC, CH, B2), bf16),
            pltpu.SMEM((4,), f32),
            pltpu.SMEM((NSEL,), jnp.int32),
            pltpu.VMEM((CH, 2 * F), bf16),
            pltpu.VMEM((1, F), f32),
            pltpu.VMEM((NP, 4, 1, B), f32),
            pltpu.SemaphoreType.DMA((NK,)),
            pltpu.SemaphoreType.DMA((NG, NP)),
            pltpu.SemaphoreType.DMA((NPC,)),
            pltpu.SemaphoreType.DMA((4,)),
            pltpu.SemaphoreType.DMA((5,)),
        ],
        compiler_params=pltpu.CompilerParams(
            collective_id=0, has_side_effects=True, vmem_limit_bytes=58 * 2**20
        ),
        cost_estimate=pl.CostEstimate(
            flops=4 * TR * TC * NA * 2 * F, bytes_accessed=4 * TR * TC * 4, transcendentals=0
        ),
        name="noise_corr",
    )(lag_weights, selected_bins, spectra, band_weights.reshape(1, F), jnp.asarray(tables()))


def solution(mesh):
    placed = (P(("rows", "cols"), None), P(), P(), P())
    return jax.shard_map(
        per_device,
        mesh=mesh,
        in_specs=placed,
        out_specs=(P(None, "rows", "cols"), P(("rows", "cols"), None)),
        check_vma=False,
    )
```

```python
import functools

import jax
import jax.numpy as jnp
import numpy as np
from jax import lax
from jax.experimental import pallas as pl
from jax.experimental.pallas import tpu as pltpu
from jax.sharding import PartitionSpec as P

MESH = pl.DeviceIdType.MESH
LAG_STEP = 8
BIN = 128
NSEL = 8
NA = 5
C = 4096
F = 2048
NP = 4
B = F // NP
B2 = 2 * B
CH = 32
TR = 2 * 4 * 2 * CH
TC = 4 * 2 * CH
EPS = 1e-05
SCALE = 1.0 / np.sqrt(2.0 * F)

NPC = NP // 2

TURN = (0, 1, 4, 2, 3)

GROUPS = {
    "ZX": "ZX", "YPO": "YO", "YMO": "YO", "YPQ": "YQ", "YMQ": "YQ", "YFO": "YF", "YFQ": "YF",
    "SB": "SB", "PM": "PM", "ZL": "ZL", "XPO": "XO", "XMO": "XO", "XPQ": "XQ", "XMQ": "XQ",
    "XFO": "XF", "XFQ": "XF", "GS": "GS", "G1P": "G1", "G1M": "G1", "G2P0": "G2", "G2P1": "G2",
    "G2M0": "G2", "G2M1": "G2", "G3": "G3", "H1P": "H1", "H1M": "H1", "H2PO": "H2",
    "H2PQ": "H2", "H2MO": "H2", "H2MQ": "H2", "H4O": "H4", "H4Q": "H4", "H5": "H5",
}
KINDS = list(GROUPS)
ARRIVALS = sorted(set(GROUPS.values()))
NK, NG = len(KINDS), len(ARRIVALS)


def tables():
    theta = np.pi * np.arange(F) * LAG_STEP / F
    rows = np.stack([np.cos(theta), np.sin(theta), np.cos(2 * theta), np.sin(2 * theta)])
    return rows.reshape(4, NP, 1, B).transpose(1, 0, 2, 3).astype(np.float32)


def kernel(
    lagw_in, bins_in, spec_in, gain_in, tab_in, corr_ref, grad_ref,
    row, col, turned, acc, short, sel, adj, adjt, part, partc,
    s_gs, r_gs, s_g1, r_g1, s_g2, r_g2, s_g3, r_g3, fin,
    s_h1, r_h1, s_h2, r_h2, s_h4, r_h4, s_h5, r_h5, lagw_ref, bins_ref, spec_ref, gain_ref, tab_ref,
    ssem, rsem, hsem, osem, isem,
):
    ins = [
        pltpu.make_async_copy(src, dst, isem.at[i])
        for i, (src, dst) in enumerate((
            (spec_in, spec_ref), (gain_in, gain_ref), (bins_in, bins_ref),
            (lagw_in, lagw_ref), (tab_in, tab_ref),
        ))
    ]
    for copy in ins:
        copy.start()
    r = lax.axis_index("rows")
    c = lax.axis_index("cols")
    x, zl, zh, y, k = r // 2, r % 2, c // 8, (c // 2) % 4, c % 2
    y1, y2, y3 = (y + 1) % 4, (y + 2) % 4, (y + 3) % 4
    x1, x3 = (x + 1) % 4, (x + 3) % 4

    def at(x_, zl_, zh_, y_, k_):
        return (x_ * 2 + zl_, zh_ * 8 + y_ * 2 + k_)

    xs, zs = c // 4, (c // 2) % 2
    kk = (zl + zs + k + 1) % 2
    yy = (x + 15 - k - 2 * kk - 3 * (xs // 2)) % 4
    yy1, yy2, yy3 = (yy + 1) % 4, (yy + 2) % 4, (yy + 3) % 4
    xt, zt = (y + zh + 2 * k + 3 * (x // 2) + 1) % 4, (zl + k + zh) % 2
    to_perm, from_perm = at(xt, 1 - zt, r // 4, r % 4, zh), at(xs, zs, k, yy, kk)
    to_mid = [at(x, zs, k, v, (k + 1 + y // 2 + v // 2) % 2) for v in (yy, yy2)]
    turn = (x + 7 - zh - y) % 4
    zm = turn % 2
    km = ((turn + 4 - 3 * zm) % 4) // 2
    ym = 2 * ((k + zh + 1 + y // 2) % 2) + zl
    xm = 2 * zm + ym // 2
    from_rep = [at(x, h, zm, ym, zh) for h in range(2)]
    home = at(xm, zl, zh, y, km)
    at_home = (xm == x) & (km == k)
    from_mid = at(xt, zl, zh, y, (zh + 1 + (r % 4) // 2 + y // 2) % 2)
    via_self = (xt == x) & ((zh + 1 + (r % 4) // 2 + y // 2) % 2 == k)
    d_zx = at(x, zl, 1 - zh, y, k)
    d_yp = at(x, zl, zh, y1, k)
    d_ym = at(x, zl, zh, y3, k)
    d_sb = at(x, zl, zh, y, 1 - k)
    d_zl = at(x, 1 - zl, zh, y, k)
    d_xp = at(x1, zl, zh, y, k)
    d_xm = at(x3, zl, zh, y, k)
    ysrc, ydst = (y + 3 + 2 * zh) % 4, (y + 1 + 2 * zh) % 4
    xsrc, xdst = (x + 3 + 2 * kk) % 4, (x + 1 + 2 * kk) % 4
    yysrc = (yy + 3 + 2 * kk) % 4
    d_ys, d_yd = at(x, zl, zh, ysrc, k), at(x, zl, zh, ydst, k)
    d_xs, d_xd = at(xsrc, zl, zh, y, k), at(xdst, zl, zh, y, k)

    barrier = pltpu.get_barrier_semaphore()
    peers = [d_zx, d_yp, d_ym, d_sb, d_zl, d_xp, d_xm, from_perm] + from_rep
    for d in peers:
        pl.semaphore_signal(barrier, inc=1, device_id=d, device_id_type=MESH)

    @pl.when(jnp.logical_not(via_self))
    def _():
        pl.semaphore_signal(barrier, inc=1, device_id=from_mid, device_id_type=MESH)

    for copy in ins:
        copy.wait()
    raw = spec_ref[...].astype(jnp.float32)
    power = jnp.mean(raw * raw, axis=1, keepdims=True)
    inv = lax.rsqrt(power + EPS)
    for p in range(NP):
        for h in range(2):
            s = slice(h * F + p * B, h * F + (p + 1) * B)
            g = gain_ref[:, p * B : (p + 1) * B]
            v = spec_ref[:, s].astype(jnp.float32) * inv * g
            row[p, zh, y, k, :, h * B : (h + 1) * B] = v.astype(jnp.bfloat16)

    pl.semaphore_wait(barrier, jnp.where(at_home, len(peers), len(peers) + 1))

    def send(kind, p, src, dst, dev):
        i = KINDS.index(kind)
        pltpu.make_async_remote_copy(
            src_ref=src, dst_ref=dst, send_sem=ssem.at[i],
            recv_sem=rsem.at[ARRIVALS.index(GROUPS[kind]), p],
            device_id=dev, device_id_type=MESH,
        ).start()

    def got(group, p, dst):
        pltpu.make_async_copy(dst, dst, rsem.at[ARRIVALS.index(group), p]).wait()

    def sent(kinds, src):
        for kind in kinds:
            pltpu.make_async_copy(src, src, ssem.at[KINDS.index(kind)]).wait()

    def run(count, table):
        for t in range(count + max(skew for _, skew in table)):
            for fn, skew in table:
                if 0 <= t - skew < count:
                    fn(t - skew)

    bits = jnp.int32(0)
    for e in range(NSEL):
        bits = bits | (jnp.int32(1) << bins_ref[e])

    def mask(p):
        def mask_rows(i, carry):
            ri = r * TR + i * 64 + lax.broadcasted_iota(jnp.int32, (64, TC), 0)
            ci = c * TC + lax.broadcasted_iota(jnp.int32, (64, TC), 1)
            dist = lax.shift_right_logical(jnp.abs(ri - ci), 7)
            hit = lax.shift_right_logical(jnp.full((64, TC), bits, jnp.int32), dist) & 1
            sel[pl.ds(pl.multiple_of(i * 64, 64), 64), :] = hit.astype(jnp.float32)
            return carry

        if p == NP - 1:
            lax.fori_loop(0, TR // 64, mask_rows, 0)

    def pair(kind, p, blk, *devs):
        for way, dev in zip("PM", devs):
            send(kind[0] + way + kind[1], p, blk, blk, dev)

    def s_start(p):
        own = row.at[p, zh, y, k]
        send("PM", p, own, col.at[p, 2, y, k], to_perm)
        send("ZX", p, own, own, d_zx)
        pair("YO", p, own, d_yp, d_ym)

    def s_perm(p):
        blk = col.at[p, 2, yy, kk]
        got("PM", p, blk)
        send("ZL", p, blk, blk, d_zl)
        pair("XO", p, blk, d_xp, d_xm)

    def s_zx(p):
        blk = row.at[p, 1 - zh, y, k]
        got("ZX", p, blk)
        pair("YQ", p, blk, d_yp, d_ym)

    def s_zl(p):
        blk = col.at[p, 2, yy2, 1 - kk]
        got("ZL", p, blk)
        pair("XQ", p, blk, d_xp, d_xm)

    def f_yo(p):
        got("YO", p, row.at[p, :, y1, k])
        blk = row.at[p, zh, ysrc, k]
        send("YFO", p, blk, blk, d_yd)

    def f_xo(p):
        got("XO", p, col.at[p, 2, yy1])
        blk = col.at[p, 2, yysrc, kk]
        send("XFO", p, blk, blk, d_xd)

    def f_yq(p):
        got("YQ", p, row.at[p, :, y1, k])
        blk = row.at[p, 1 - zh, ydst, k]
        send("YFQ", p, blk, blk, d_ys)

    def f_xq(p):
        got("XQ", p, col.at[p, 2, yy1])
        blk = col.at[p, 2, yysrc, 1 - kk]
        send("XFQ", p, blk, blk, d_xs)

    def s_sib(p):
        got("YF", p, row.at[p, :, y2, k])
        blk = row.at[p, :, :, k]
        send("SB", p, blk, blk, d_sb)

    def g_xf(p):
        got("XF", p, col.at[p, 2, yy2])

    def g_sib(p):
        got("SB", p, row.at[p, :, :, 1 - k])

    def rotate(p, v, put):
        re = v[:, :B].astype(jnp.float32)
        im = v[:, B:].astype(jnp.float32)
        for t in range(2):
            cs, sn = tab_ref[p, 2 * t], tab_ref[p, 2 * t + 1]
            rc, rs, ic, is_ = re * cs, re * sn, im * cs, im * sn
            put(t, 0, (rc - is_).astype(jnp.bfloat16), (ic + rs).astype(jnp.bfloat16))
            put(t, 1, (rc + is_).astype(jnp.bfloat16), (ic - rs).astype(jnp.bfloat16))

    def rot(p):
        def body(i, carry):
            a, b = i // 2, i % 2

            def put(t, back, re, im):
                o = ((1, 3), (0, 4))[t][back]
                col[p, o, a, b, :, :B] = re
                col[p, o, a, b, :, B:] = im

            rotate(p, col[p, 2, a, b], put)
            return carry

        lax.fori_loop(0, 8, body, 0)

    def rot_first(p):
        def body(i, carry):
            h, a, b = i // 8, (i // 2) % 4, i % 2

            def put(t, back, re, im):
                o = ((2, 1), (3, 0))[t][back]
                turned[p, o, h, a, b, :, :B] = re
                turned[p, o, h, a, b, :, B:] = im

            rotate(p, row[p, h, a, b], put)
            return carry

        if p < NPC:
            lax.fori_loop(0, 16, body, 0)

    def correlate(p):
        left = row[p].reshape(TR, B2)
        for a in range(NA):
            d = lax.dot_general(
                left, col[p, a].reshape(TC, B2), (((1,), (1,)), ((), ())),
                preferred_element_type=jnp.float32,
            )
            if p > 0:
                d = acc[a] + d
            if p < NP - 1:
                acc[a] = d
                continue
            d = d * jnp.float32(SCALE)
            if a < 4:
                short[a] = d.astype(jnp.bfloat16)
                outs[a].start()
            d = (d * (sel[...] * weights[a])).astype(jnp.bfloat16)
            adj[:, a * TC : (a + 1) * TC] = d
            adjt[TURN[a] * TR : (TURN[a] + 1) * TR, :] = d

    outs = [pltpu.make_async_copy(short.at[a], corr_ref.at[a], osem.at[a]) for a in range(4)]
    w0, w8, w16 = 2.0 * lagw_ref[2], lagw_ref[1] + lagw_ref[3], lagw_ref[0]
    weights = (w16, w8, w0, w8, w16)
    run(NP, [
        (s_start, 0), (mask, 0), (s_perm, 1), (s_zx, 1), (f_yo, 1), (s_zl, 2), (f_xo, 2), (f_yq, 2),
        (f_xq, 3), (s_sib, 3), (g_xf, 4), (rot, 4), (g_sib, 4), (correlate, 4), (rot_first, 4),
    ])

    def f32(v):
        return v.astype(jnp.float32)

    def b16(v):
        return v.astype(jnp.bfloat16)

    def grad0(q):
        p = NPC + q

        d = jnp.dot(
            adj[...], col[p].reshape(NA * TC, B2), preferred_element_type=jnp.float32
        )
        part[q] = d.reshape(2, 4, 2, CH, B2)
        s_gs[q] = b16(part[q, :, :, 1 - k])
        send("GS", q, s_gs.at[q], r_gs.at[q], d_sb)

    def mine_at(q, h, yt):
        return part[q, h, yt, k] + f32(r_gs[q, h, yt])

    def reach(kind, q, src, dst, value, dev):
        src[...] = b16(value)
        send(kind, q, src, dst, dev)

    def grad1(q):
        got("GS", q, r_gs.at[q])
        reach("G1P", q, s_g1.at[q, 0], r_g1.at[q, 0], mine_at(q, 0, y2), d_yp)
        reach("G1M", q, s_g1.at[q, 1], r_g1.at[q, 1], mine_at(q, 1, y2), d_ym)
        reach("G2P1", q, s_g2.at[q, 0, 1], r_g2.at[q, 0, 1], mine_at(q, 1, y1), d_yp)
        reach("G2M0", q, s_g2.at[q, 1, 0], r_g2.at[q, 1, 0], mine_at(q, 0, y3), d_ym)

    def grad2(q):
        got("G1", q, r_g1.at[q])
        v = mine_at(q, 0, y1) + f32(r_g1[q, 0])
        reach("G2P0", q, s_g2.at[q, 0, 0], r_g2.at[q, 0, 0], v, d_yp)
        v = mine_at(q, 1, y3) + f32(r_g1[q, 1])
        reach("G2M1", q, s_g2.at[q, 1, 1], r_g2.at[q, 1, 1], v, d_ym)

    def grad3(q):
        def total_at(h):
            return mine_at(q, h, y) + f32(r_g2[q, 0, h]) + f32(r_g2[q, 1, h])

        got("G2", q, r_g2.at[q])
        s_g3[q] = b16(total_at(1 - zh))
        send("G3", q, s_g3.at[q], r_g3.at[q], d_zx)
        fin[q] = total_at(zh)

    def put_grad(p, v):
        v = v * jnp.float32(SCALE)
        grad_ref[:, p * B : (p + 1) * B] = v[:, :B]
        grad_ref[:, F + p * B : F + (p + 1) * B] = v[:, B:]

    def grad4(q):
        got("G3", q, r_g3.at[q])
        put_grad(NPC + q, fin[q] + f32(r_g3[q]))

    def colg0(q):
        def turned_dot(lags, right):
            return lax.dot_general(
                lags, right, (((0,), (0,)), ((), ())), preferred_element_type=jnp.float32
            )

        d = turned_dot(adjt[: 4 * TR, :], turned[q].reshape(4 * TR, B2))
        d += turned_dot(adjt[4 * TR :, :], row[q].reshape(TR, B2))
        partc[q] = d.reshape(4, 2, CH, B2)
        reach("H1P", q, s_h1.at[q, 0], r_h1.at[q, 0], partc[q, yy2, kk], d_xp)
        reach("H1M", q, s_h1.at[q, 1], r_h1.at[q, 1], partc[q, yy, 1 - kk], d_xm)
        reach("H2PQ", q, s_h2.at[q, 0, 1], r_h2.at[q, 0, 1], partc[q, yy3, 1 - kk], d_xp)
        reach("H2MO", q, s_h2.at[q, 1, 0], r_h2.at[q, 1, 0], partc[q, yy3, kk], d_xm)

    def colg1(q):
        got("H1", q, r_h1.at[q])
        v = partc[q, yy1, kk] + f32(r_h1[q, 0])
        reach("H2PO", q, s_h2.at[q, 0, 0], r_h2.at[q, 0, 0], v, d_xp)
        v = partc[q, yy1, 1 - kk] + f32(r_h1[q, 1])
        reach("H2MQ", q, s_h2.at[q, 1, 1], r_h2.at[q, 1, 1], v, d_xm)

    def colg2(q):
        got("H2", q, r_h2.at[q])
        v = partc[q, yy, kk] + f32(r_h2[q, 0, 0]) + f32(r_h2[q, 1, 0])
        reach("H4O", q, s_h4.at[q, 0], r_h4.at[q, 0], v, to_mid[0])
        v = partc[q, yy2, 1 - kk] + f32(r_h2[q, 0, 1]) + f32(r_h2[q, 1, 1])
        reach("H4Q", q, s_h4.at[q, 1], r_h4.at[q, 1], v, to_mid[1])

    def homeward(q):
        return pltpu.make_async_remote_copy(
            src_ref=s_h5.at[q], dst_ref=r_h5.at[q], send_sem=hsem.at[q],
            recv_sem=rsem.at[ARRIVALS.index("H5"), q], device_id=home, device_id_type=MESH,
        )

    def colg3(q):
        got("H4", q, r_h4.at[q])
        s_h5[q] = b16(f32(r_h4[q, 0]) + f32(r_h4[q, 1]))

        @pl.when(at_home)
        def _():
            r_h5[q] = s_h5[q]

        @pl.when(jnp.logical_not(at_home))
        def _():
            homeward(q).start()

    def colg4(q):
        @pl.when(jnp.logical_not(at_home))
        def _():
            homeward(q).wait_send()

        @pl.when(jnp.logical_not(via_self))
        def _():
            got("H5", q, r_h5.at[q])

        put_grad(q, f32(r_h5[q]))

    def settle():
        for kind in KINDS[: KINDS.index("GS")]:
            sent([kind], row.at[:, :, :, k] if kind == "SB" else row.at[:, zh, y, k])
        for o in outs:
            o.wait()

    for q in range(NPC):
        colg0(q)
        grad0(q)
    for n, fns in enumerate(((colg1, grad1), (colg2, grad2), (colg3, grad3), (colg4, grad4))):
        for q in range(NPC):
            for fn in fns:
                fn(q)
        if n == 0:
            settle()

    for kind in KINDS[KINDS.index("GS") : KINDS.index("H5")]:
        sent([kind], s_gs if kind == "GS" else s_h1.at[:, 0])


def per_device(spectra, band_weights, lag_weights, selected_bins):
    bf16, f32 = jnp.bfloat16, jnp.float32
    hbm = pl.BlockSpec(memory_space=pltpu.HBM)
    vmem = pl.BlockSpec(memory_space=pltpu.VMEM)
    corr, grad = pl.pallas_call(
        kernel,
        out_shape=(
            jax.ShapeDtypeStruct((4, TR, TC), bf16),
            jax.ShapeDtypeStruct((CH, 2 * F), f32),
        ),
        in_specs=[hbm] * 5,
        out_specs=(pl.BlockSpec(memory_space=pl.ANY), vmem),
        scratch_shapes=[
            pltpu.VMEM((NP, 2, 4, 2, CH, B2), bf16),
            pltpu.VMEM((NP, NA, 4, 2, CH, B2), bf16),
            pltpu.VMEM((NPC, 4, 2, 4, 2, CH, B2), bf16),
            pltpu.VMEM((NA, TR, TC), f32),
            pltpu.VMEM((4, TR, TC), bf16),
            pltpu.VMEM((TR, TC), f32),
            pltpu.VMEM((TR, NA * TC), bf16),
            pltpu.VMEM((NA * TR, TC), bf16),
            pltpu.VMEM((NPC, 2, 4, 2, CH, B2), f32),
            pltpu.VMEM((NPC, 4, 2, CH, B2), f32),
            pltpu.VMEM((NPC, 2, 4, CH, B2), bf16),
            pltpu.VMEM((NPC, 2, 4, CH, B2), bf16),
            pltpu.VMEM((NPC, 2, CH, B2), bf16),
            pltpu.VMEM((NPC, 2, CH, B2), bf16),
            pltpu.VMEM((NPC, 2, 2, CH, B2), bf16),
            pltpu.VMEM((NPC, 2, 2, CH, B2), bf16),
            pltpu.VMEM((NPC, CH, B2), bf16),
            pltpu.VMEM((NPC, CH, B2), bf16),
            pltpu.VMEM((NPC, CH, B2), f32),
            pltpu.VMEM((NPC, 2, CH, B2), bf16),
            pltpu.VMEM((NPC, 2, CH, B2), bf16),
            pltpu.VMEM((NPC, 2, 2, CH, B2), bf16),
            pltpu.VMEM((NPC, 2, 2, CH, B2), bf16),
            pltpu.VMEM((NPC, 2, CH, B2), bf16),
            pltpu.VMEM((NPC, 2, CH, B2), bf16),
            pltpu.VMEM((NPC, CH, B2), bf16),
            pltpu.VMEM((NPC, CH, B2), bf16),
            pltpu.SMEM((4,), f32),
            pltpu.SMEM((NSEL,), jnp.int32),
            pltpu.VMEM((CH, 2 * F), bf16),
            pltpu.VMEM((1, F), f32),
            pltpu.VMEM((NP, 4, 1, B), f32),
            pltpu.SemaphoreType.DMA((NK,)),
            pltpu.SemaphoreType.DMA((NG, NP)),
            pltpu.SemaphoreType.DMA((NPC,)),
            pltpu.SemaphoreType.DMA((4,)),
            pltpu.SemaphoreType.DMA((5,)),
        ],
        compiler_params=pltpu.CompilerParams(
            collective_id=0, has_side_effects=True, vmem_limit_bytes=58 * 2**20
        ),
        cost_estimate=pl.CostEstimate(
            flops=4 * TR * TC * NA * 2 * F, bytes_accessed=4 * TR * TC * 4, transcendentals=0
        ),
        name="noise_corr",
    )(lag_weights, selected_bins, spectra, band_weights.reshape(1, F), jnp.asarray(tables()))
    return corr.astype(f32), grad


def solution(mesh):
    placed = (P(("rows", "cols"), None), P(), P(), P())
    return jax.shard_map(
        per_device,
        mesh=mesh,
        in_specs=placed,
        out_specs=(P(None, "rows", "cols"), P(("rows", "cols"), None)),
        check_vma=False,
    )
```
